32 devices in a mesh: src: 8 (over z, core), loop: 4 (over y, x).
Axes of the slice: x: 2, y: 2, z: 4, core: 2. Of those that a mesh axis runs over, the one named last changes fastest.
Arguments:
- sources: bfloat16 [16384, 768], P(('src', 'loop')), may hold values from -48 to 48
- log_a: float32 [16384], P(('src', 'loop')), may hold values from -3 to 0
- targets: bfloat16 [64, 512, 768], P('src'), may hold values from -6 to 6
- g_old: bfloat16 [64, 512], P('src'), may hold values from -2.5 to 2.5
- log_b: float32 [64, 512], P('src'), may hold values from -3 to 0
- tile_ids: int32 [32, 8, 2], P(('src', 'loop')), may hold values from 0 to 63, as said below
- live_count: int32 [32, 8], P(('src', 'loop')), may hold values from 1 to 2, as said below
Outputs:
- f_new: float32 [16384], P(('src', 'loop'))
- g_new: float32 [64, 512], P('src')
The draws below stay inside these ranges and needn't reach their ends.
Inputs may be any that keep to these rules, and one draw needn't show every extreme that they name: `tile_ids`: tile ids of one device for index o of src lie in o * 8 to (o + 1) * 8 - 1 and are distinct within that group of 2 slots; every tile is in use in some device's list. `live_count`: every index of src has a full group of 2 slots in use in some device's list.
All inputs are finite; a program needn't handle non-finite values.
Results may differ from the reference program's by a relative error of at most 0.0003.
Values may be sent and summed in bfloat16 or wider, within the bound.
A program may use at most 128 MiB of HBM per device.

```python
import math
import jax
import jax.numpy as jnp
from jax import lax

D = 768
ROWS = 512
TILE = 512
TILES_OWN = 8
CAP = 2
SOURCES = 16384
NT = 64
N_SRC = 8
DEVICES = 32


def draw_sources(key, part):
    key_values = jax.random.fold_in(key, 0)
    values = jnp.clip(jax.random.normal(key_values, (SOURCES, D), jnp.float32), -6.0, 6.0)
    return values.astype(jnp.bfloat16)


def draw_tile_ids(key, part):
    key_order, key_offset, key_stride = jax.random.split(jax.random.fold_in(key, 11), 3)
    order = jax.random.permutation(key_order, DEVICES)
    offset = jax.random.randint(key_offset, (N_SRC,), 0, TILES_OWN)
    stride = 2 * jax.random.randint(key_stride, (DEVICES, N_SRC), 0, TILES_OWN // 2) + 1
    base = (order[:, None] + offset[None, :]) % TILES_OWN
    slots = jnp.arange(CAP, dtype=jnp.int32)
    local = (base[:, :, None] + slots[None, None, :] * stride[:, :, None]) % TILES_OWN
    owner = jnp.arange(N_SRC, dtype=jnp.int32)
    return (owner[None, :, None] * TILES_OWN + local).astype(jnp.int32)


def draw_live_count(key, part):
    counts = jax.random.randint(jax.random.fold_in(key, 23), (DEVICES, N_SRC), 1, CAP + 1)
    full = jnp.arange(DEVICES)[:, None] % N_SRC == jnp.arange(N_SRC)[None, :]
    return jnp.where(full, CAP, counts).astype(jnp.int32)


def level_of(own_key, shape, cuts, smallest, largest):
    gain = 1.0
    for dim, blocks in cuts:
        steps = jax.random.uniform(jax.random.fold_in(jax.random.fold_in(own_key, 6), dim), (blocks,), jnp.float32, smallest / len(cuts), largest / len(cuts))
        gain = gain * jnp.repeat(jnp.exp(steps), shape[dim] // blocks).reshape((-1,) + (1,) * (len(shape) - 1 - dim))
    return gain


def scatter_about(rng, extent, width, limit, pieces=(), kind=jnp.bfloat16):
    gain = level_of(rng, extent, pieces, -0.22, 0.18) if pieces else 1.0
    values = jax.random.normal(rng, extent, jnp.float32) * width * gain
    return jnp.minimum(jnp.maximum(values, -limit), limit).astype(kind)


def setup_inputs(seed: int = 0) -> dict:
    keys = jax.random.split(jax.random.key(seed), 8)
    sources = draw_sources(jax.random.fold_in(keys[7], 71), 0)
    log_a = jnp.clip(-3.0 + 3.0 * jax.random.uniform(keys[1], (SOURCES,), jnp.float32) ** level_of(keys[1], (SOURCES,), ((0, 32),), -0.2, 0.2), -3.0, 0.0)
    targets = scatter_about(keys[2], (NT, TILE, D), 1.0, 6.0, ((0, 8),))
    g_old = scatter_about(keys[3], (NT, TILE), 0.3, 2.5, ((0, 8),))
    log_b = jnp.clip(-3.0 + 3.0 * jax.random.uniform(keys[4], (NT, TILE), jnp.float32) ** level_of(keys[4], (NT, TILE), ((0, 8),), -0.2, 0.2), -3.0, 0.0)
    tile_ids = draw_tile_ids(jax.random.fold_in(keys[7], 71), 0)
    live_count = draw_live_count(jax.random.fold_in(keys[7], 71), 0)
    return dict(sources=sources, log_a=log_a, targets=targets, g_old=g_old, log_b=log_b, tile_ids=tile_ids, live_count=live_count)


EPSILON = 0.1
VERY_LOW = -1e+30

def similarity(rows, fetched):
    return jnp.einsum('rd,std->rst', rows.astype(jnp.float32), fetched.astype(jnp.float32)) / math.sqrt(D)

def reference(sources, log_a, targets, g_old, log_b, tile_ids, live_count):
    source_blocks = sources.reshape(DEVICES, ROWS, D)
    mass_blocks = log_a.reshape(DEVICES, ROWS)
    id_blocks = tile_ids.reshape(DEVICES, N_SRC * CAP).astype(jnp.int32)
    slot_index = jnp.arange(CAP, dtype=jnp.int32)
    live_blocks = (slot_index[None, None, :] < live_count[:, :, None]).reshape(DEVICES, N_SRC * CAP)
    potential = g_old.astype(jnp.float32)

    def row_step(item):
        rows, masses, idents, live_slots = item
        kernel = similarity(rows, targets[idents])
        logits = (potential[idents][None] + kernel) / EPSILON
        logits = jnp.where(live_slots[None, :, None], logits, VERY_LOW)
        top = lax.optimization_barrier(jnp.max(logits, axis=(1, 2)))
        total = lax.optimization_barrier(jnp.sum(jnp.exp(logits - top[:, None, None]), axis=(1, 2)))
        return EPSILON * masses - EPSILON * (top + jnp.log(total))
    f_blocks = lax.map(row_step, (source_blocks, mass_blocks, id_blocks, live_blocks))

    def column_step(carry, item):
        col_top, col_total = carry
        rows, row_potential, idents, live_slots = item
        kernel = similarity(rows, targets[idents])
        logits = (row_potential[:, None, None] + kernel) / EPSILON
        top = lax.optimization_barrier(jnp.max(logits, axis=0))
        total = lax.optimization_barrier(jnp.sum(jnp.exp(logits - top[None]), axis=0))
        top = jnp.where(live_slots[:, None], top, VERY_LOW)
        total = jnp.where(live_slots[:, None], total, 0.0)
        old_top = col_top[idents]
        new_top = jnp.maximum(old_top, top)
        new_total = col_total[idents] * jnp.exp(old_top - new_top) + total * jnp.exp(top - new_top)
        return ((col_top.at[idents].set(new_top), col_total.at[idents].set(new_total)), None)
    start = (jnp.full((NT, TILE), VERY_LOW, jnp.float32), jnp.zeros((NT, TILE), jnp.float32))
    (col_top, col_total), unused = lax.scan(column_step, start, (source_blocks, f_blocks, id_blocks, live_blocks))
    g_new = EPSILON * log_b - EPSILON * (col_top + jnp.log(col_total))
    return (f_blocks.reshape(SOURCES), g_new)
```

```python
import functools
import math

import jax
import jax.numpy as jnp
from jax import lax
from jax.experimental import pallas as pl
from jax.experimental.pallas import tpu as pltpu
from jax.sharding import PartitionSpec as P

EPSILON = 0.1
VERY_LOW = -1e30
LOG2E = math.log2(math.e)
LN2 = math.log(2.0)
CHUNKS = 2
MESH = pl.DeviceIdType.MESH


def fused(
    n_src, n_loop, slots,
    src_ref, tgt_ref, log_a_ref, g_old_ref, log_b_ref, idpack_ref,
    f_ref, g_ref,
    gather, tiles, logits, gcol, ids_v, ids_s, row_out, row_in, f_all,
    col_top, col_sum, loop_out, loop_in,
    gs_send, gs_recv, id_send, id_recv, row_send, row_recv, f_send, f_recv,
    loop_send, loop_recv, loc_sem,
):
    rows, depth = src_ref.shape
    tiles_own, width, _ = tgt_ref.shape
    chunk = rows // CHUNKS
    n_chip = n_src // 2
    scale = LOG2E / (EPSILON * math.sqrt(depth))
    me = lax.axis_index("src")
    ml = lax.axis_index("loop")
    chip = me // 2
    core = me % 2
    sib = chip * 2 + (1 - core)

    def at_src(s):
        return (s, ml)

    def peer(k):
        return lax.rem(me + k, n_src)

    def loop_peer(k):
        return lax.rem(ml + k, n_loop)

    tile_copy = pltpu.make_async_copy(tgt_ref, tiles, loc_sem.at[0])
    own_copy = pltpu.make_async_copy(src_ref, gather.at[me], loc_sem.at[1])
    own_ids = pltpu.make_async_copy(idpack_ref.at[me], ids_v.at[me], loc_sem.at[2])
    tile_copy.start()
    own_copy.start()
    own_ids.start()

    barrier = pltpu.get_barrier_semaphore()
    for k in range(1, n_src):
        pl.semaphore_signal(barrier, inc=1, device_id=(peer(k), ml), device_id_type=MESH)
    for k in range(1, n_loop):
        pl.semaphore_signal(barrier, inc=1, device_id=(me, loop_peer(k)), device_id_type=MESH)
    pl.semaphore_wait(barrier, n_src - 1 + n_loop - 1)

    def id_copy(to, slot):
        return pltpu.make_async_remote_copy(
            src_ref=idpack_ref.at[to], dst_ref=ids_v.at[slot],
            send_sem=id_send.at[to], recv_sem=id_recv.at[slot],
            device_id=at_src(to), device_id_type=MESH,
        )

    for k in range(1, n_src):
        id_copy(peer(k), me).start()

    def own_send(ch, lane, to):
        part = pl.ds(ch * chunk, chunk)
        return pltpu.make_async_remote_copy(
            src_ref=src_ref.at[part], dst_ref=gather.at[me, part],
            send_sem=gs_send.at[me, ch, lane], recv_sem=gs_recv.at[me, ch],
            device_id=at_src(to), device_id_type=MESH,
        )

    def pass_on(block, ch, lane, to):
        part = pl.ds(ch * chunk, chunk)
        return pltpu.make_async_remote_copy(
            src_ref=gather.at[block, part], dst_ref=gather.at[block, part],
            send_sem=gs_send.at[block, ch, lane], recv_sem=gs_recv.at[block, ch],
            device_id=at_src(to), device_id_type=MESH,
        )

    up = lax.rem(me + 2, n_src)
    down = lax.rem(me + n_src - 2, n_src)
    has_up = chip < n_chip - 1
    has_down = chip > 0
    for ch in range(CHUNKS):
        @pl.when(has_up)
        def _():
            own_send(ch, 0, up).start()

        @pl.when(has_down)
        def _():
            own_send(ch, 1, down).start()

    for ch in range(CHUNKS):
        own_send(ch, 2, sib).start()

    def fill(t, carry):
        row = g_old_ref[t] * (LOG2E / EPSILON)
        gcol[t] = jnp.broadcast_to(row, (128, width)).T
        return carry

    lax.fori_loop(0, tiles_own, fill, 0)

    own_ids.wait()
    for k in range(1, n_src):
        id_copy(peer(k), peer(k)).wait_recv()
    to_smem = pltpu.make_async_copy(ids_v, ids_s, loc_sem.at[3])
    to_smem.start()
    to_smem.wait()
    tile_copy.wait()
    own_copy.wait()

    def row_copy(to, slot):
        return pltpu.make_async_remote_copy(
            src_ref=row_out.at[to], dst_ref=row_in.at[slot],
            send_sem=row_send.at[to], recv_sem=row_recv.at[slot],
            device_id=at_src(to), device_id_type=MESH,
        )

    def row_part(block, ch):
        part = pl.ds(pl.multiple_of(ch * chunk, chunk), chunk)
        rows_bf = gather[block, part, :]
        live = ids_s[block, 0, slots]
        best = None
        for c in range(slots):
            tid = ids_s[block, 0, c]
            dots = lax.dot_general(
                tiles[tid], rows_bf, (((1,), (1,)), ((), ())),
                preferred_element_type=jnp.float32,
            )
            g_rows = gcol[tid]
            vals = dots * scale + jnp.concatenate([g_rows] * (chunk // 128), axis=1)
            logits[block * slots + c, :, part] = vals
            top = jnp.max(vals, axis=0, keepdims=True)
            total = jnp.sum(jnp.exp2(vals - top), axis=0, keepdims=True)
            if c == 0:
                best, tot = top, total
            else:
                top = jnp.where(c < live, top, VERY_LOW)
                total = jnp.where(c < live, total, 0.0)
                new = jnp.maximum(best, top)
                tot = tot * jnp.exp2(best - new) + total * jnp.exp2(top - new)
                best = new
        row_out[block, 0:1, part] = best
        row_out[block, 1:2, part] = tot

    def own_step(ch, carry):
        row_part(me, ch)
        return carry

    lax.fori_loop(0, CHUNKS, own_step, 0)
    row_in[me] = row_out[me]

    def sib_step(ch, carry):
        pass_on(sib, ch, 2, sib).wait_recv()
        row_part(sib, ch)
        return carry

    lax.fori_loop(0, CHUNKS, sib_step, 0)
    row_copy(sib, me).start()

    def chip_step(k, carry):
        low = chip - k
        high = chip + k

        def chunk_step(ch, carry):
            @pl.when(low >= 0)
            def _():
                block = low * 2 + core
                pass_on(block, ch, 0, up).wait_recv()

                @pl.when(has_up)
                def _():
                    pass_on(block, ch, 0, up).start()

                pass_on(block, ch, 2, sib).start()

            @pl.when(high < n_chip)
            def _():
                block = high * 2 + core
                pass_on(block, ch, 1, down).wait_recv()

                @pl.when(has_down)
                def _():
                    pass_on(block, ch, 1, down).start()

                pass_on(block, ch, 2, sib).start()

            def part_step(j, carry):
                other = jnp.where(j % 2 == 0, low, high)
                own_core = j < 2

                @pl.when((other >= 0) & (other < n_chip))
                def _():
                    block = other * 2 + jnp.where(own_core, core, 1 - core)

                    @pl.when(jnp.logical_not(own_core))
                    def _():
                        pass_on(block, ch, 2, sib).wait_recv()

                    row_part(block, ch)

                    @pl.when(ch == CHUNKS - 1)
                    def _():
                        row_copy(block, me).start()

                return carry

            return lax.fori_loop(0, 4, part_step, carry)

        return lax.fori_loop(0, CHUNKS, chunk_step, carry)

    lax.fori_loop(1, n_chip, chip_step, 0)

    for k in range(1, n_src):
        row_copy(peer(k), peer(k)).wait_recv()
    tops = row_in[:, 0, :]
    best = jnp.max(tops, axis=0, keepdims=True)
    total = jnp.sum(row_in[:, 1, :] * jnp.exp2(tops - best), axis=0, keepdims=True)
    f_two = log_a_ref[...] * LOG2E - (best + jnp.log2(total))
    f_ref[...] = f_two * (EPSILON * LN2)
    f_all[me] = f_two

    def f_copy(to, slot):
        return pltpu.make_async_remote_copy(
            src_ref=f_all.at[slot], dst_ref=f_all.at[slot],
            send_sem=f_send.at[to], recv_sem=f_recv.at[slot],
            device_id=at_src(to), device_id_type=MESH,
        )

    for k in range(1, n_src):
        f_copy(peer(k), me).start()
    for k in range(1, n_src):
        f_copy(peer(k), peer(k)).wait_recv()

    n_pairs = n_src * slots
    band = 32
    lane = lax.broadcasted_iota(jnp.int32, (band, 128), 1)

    def band_step(r, carry):
        at = pl.ds(pl.multiple_of(r * band, band), band)

        def pair_step(p, state):
            tops, sums = state
            vals = logits[p, at, :] + f_all[p // slots]
            parts = [vals[:, i : i + 128] for i in range(0, rows, 128)]
            top = functools.reduce(jnp.maximum, parts)
            total = functools.reduce(jnp.add, [jnp.exp2(v - top) for v in parts])
            full = jnp.max(top, axis=1, keepdims=True)
            total = jnp.sum(total * jnp.exp2(top - full), axis=1, keepdims=True)
            return (jnp.where(lane == p, full, tops), jnp.where(lane == p, total, sums))

        zero = jnp.zeros((band, 128), jnp.float32)
        tops, sums = lax.fori_loop(0, n_pairs, pair_step, (zero, zero), unroll=4)
        col_top[at, :] = tops
        col_sum[at, :] = sums
        return carry

    lax.fori_loop(0, width // band, band_step, 0)
    tops = col_top[...].T
    sums = col_sum[...].T
    index = lax.broadcasted_iota(jnp.int32, (tiles_own, width), 0)
    masks = []
    tile_top = jnp.full((tiles_own, width), VERY_LOW, jnp.float32)
    for p in range(n_pairs):
        block, c = p // slots, p % slots
        tid = jnp.where(c < ids_s[block, 0, slots], ids_s[block, 0, c], -1)
        mask = index == tid
        masks.append(mask)
        tile_top = jnp.maximum(tile_top, jnp.where(mask, tops[p : p + 1], VERY_LOW))
    tile_sum = jnp.zeros((tiles_own, width), jnp.float32)
    for p in range(n_pairs):
        term = sums[p : p + 1] * jnp.exp2(jnp.minimum(tops[p : p + 1] - tile_top, 0.0))
        tile_sum = tile_sum + jnp.where(masks[p], term, 0.0)

    loop_in[ml, 0] = tile_top
    loop_in[ml, 1] = tile_sum
    loop_out[0] = tile_top
    loop_out[1] = tile_sum

    def loop_copy(to, slot):
        return pltpu.make_async_remote_copy(
            src_ref=loop_out, dst_ref=loop_in.at[slot],
            send_sem=loop_send.at[to], recv_sem=loop_recv.at[slot],
            device_id=(me, to), device_id_type=MESH,
        )

    for k in range(1, n_loop):
        loop_copy(loop_peer(k), ml).start()
    for k in range(1, n_loop):
        loop_copy(loop_peer(k), loop_peer(k)).wait_recv()
    top = functools.reduce(jnp.maximum, [loop_in[i, 0] for i in range(n_loop)])
    total = functools.reduce(
        jnp.add, [loop_in[i, 1] * jnp.exp2(loop_in[i, 0] - top) for i in range(n_loop)]
    )
    g_ref[...] = (
        EPSILON * log_b_ref[...] - (EPSILON * LN2) * (top + jnp.log2(total)) + g_old_ref[:, 0, :]
    )

    for k in range(1, n_loop):
        loop_copy(loop_peer(k), ml).wait_send()
    for k in range(1, n_src):
        f_copy(peer(k), me).wait_send()
        row_copy(peer(k), me).wait_send()
        id_copy(peer(k), me).wait_send()
    for ch in range(CHUNKS):
        @pl.when(has_up)
        def _():
            own_send(ch, 0, up).wait_send()

        @pl.when(has_down)
        def _():
            own_send(ch, 1, down).wait_send()

        own_send(ch, 2, sib).wait_send()

    def drain(k, carry):
        low = chip - k
        high = chip + k
        for ch in range(CHUNKS):
            @pl.when(low >= 0)
            def _():
                block = low * 2 + core

                @pl.when(has_up)
                def _():
                    pass_on(block, ch, 0, up).wait_send()

                pass_on(block, ch, 2, sib).wait_send()

            @pl.when(high < n_chip)
            def _():
                block = high * 2 + core

                @pl.when(has_down)
                def _():
                    pass_on(block, ch, 1, down).wait_send()

                pass_on(block, ch, 2, sib).wait_send()

        return carry

    lax.fori_loop(1, n_chip, drain, 0)


def local(sources, log_a, targets, g_old, log_b, tile_ids, live_count):
    n_src = lax.axis_size("src")
    n_loop = lax.axis_size("loop")
    rows, depth = sources.shape
    tiles_own, width = targets.shape[0], targets.shape[1]
    slots = tile_ids.shape[2]
    base = jnp.arange(n_src, dtype=jnp.int32) * tiles_own
    listed = jnp.concatenate([tile_ids[0] - base[:, None], live_count[0][:, None]], axis=1)
    idpack = jnp.pad(listed, ((0, 0), (0, 128 - slots - 1)))[:, None, :]
    vmem = pl.BlockSpec(memory_space=pltpu.VMEM)
    hbm = pl.BlockSpec(memory_space=pl.ANY)
    dma = pltpu.SemaphoreType.DMA
    n_pairs = n_src * slots
    f_new, g_new = pl.pallas_call(
        functools.partial(fused, n_src, n_loop, slots),
        out_shape=(
            jax.ShapeDtypeStruct((1, rows), jnp.float32),
            jax.ShapeDtypeStruct((tiles_own, width), jnp.float32),
        ),
        in_specs=[hbm, hbm, vmem, vmem, vmem, vmem],
        out_specs=(vmem, vmem),
        scratch_shapes=[
            pltpu.VMEM((n_src, rows, depth), sources.dtype),
            pltpu.VMEM((tiles_own, width, depth), targets.dtype),
            pltpu.VMEM((n_pairs, width, rows), jnp.float32),
            pltpu.VMEM((tiles_own, width, 128), jnp.float32),
            pltpu.VMEM((n_src, 1, 128), jnp.int32),
            pltpu.SMEM((n_src, 1, 128), jnp.int32),
            pltpu.VMEM((n_src, 2, rows), jnp.float32),
            pltpu.VMEM((n_src, 2, rows), jnp.float32),
            pltpu.VMEM((n_src, 1, rows), jnp.float32),
            pltpu.VMEM((width, 128), jnp.float32),
            pltpu.VMEM((width, 128), jnp.float32),
            pltpu.VMEM((2, tiles_own, width), jnp.float32),
            pltpu.VMEM((n_loop, 2, tiles_own, width), jnp.float32),
            dma((n_src, CHUNKS, 3)),
            dma((n_src, CHUNKS)),
            dma((n_src,)),
            dma((n_src,)),
            dma((n_src,)),
            dma((n_src,)),
            dma((n_src,)),
            dma((n_src,)),
            dma((n_loop,)),
            dma((n_loop,)),
            dma((4,)),
        ],
        compiler_params=pltpu.CompilerParams(
            collective_id=0, has_side_effects=True, vmem_limit_bytes=60 * 1024 * 1024
        ),
        cost_estimate=pl.CostEstimate(
            flops=2 * n_pairs * rows * width * depth,
            bytes_accessed=2 * (tiles_own * width + rows) * depth,
            transcendentals=2 * n_pairs * rows * width,
        ),
    )(
        sources,
        targets,
        log_a[None],
        g_old.astype(jnp.float32)[:, None, :],
        log_b,
        idpack,
    )
    return (f_new[0], g_new)


def solution(mesh):
    return jax.shard_map(
        local,
        mesh=mesh,
        in_specs=(
            P(("src", "loop"), None),
            P(("src", "loop")),
            P("src", None, None),
            P("src", None),
            P("src", None),
            P(("src", "loop"), None, None),
            P(("src", "loop"), None),
        ),
        out_specs=(P(("src", "loop")), P("src", None)),
        check_vma=False,
    )
```

```python
import functools
import math

import jax
import jax.numpy as jnp
from jax import lax
from jax.experimental import pallas as pl
from jax.experimental.pallas import tpu as pltpu
from jax.sharding import PartitionSpec as P

EPSILON = 0.1
VERY_LOW = -1e30
LOG2E = math.log2(math.e)
LN2 = math.log(2.0)
CHUNKS = 2
MESH = pl.DeviceIdType.MESH


def fused(
    n_src, n_loop, slots,
    src_ref, tgt_ref, log_a_ref, g_old_ref, log_b_ref, list_ref, live_ref,
    f_ref, g_ref,
    gather, tiles, logits, gcol, idpack_ref, ids_v, ids_s, row_out, row_in, f_all,
    col_top, col_sum, loop_out, loop_in,
    gs_send, gs_recv, id_send, id_recv, row_send, row_recv, f_send, f_recv,
    loop_send, loop_recv, loc_sem,
):
    rows, depth = src_ref.shape
    tiles_own, width, _ = tgt_ref.shape
    chunk = rows // CHUNKS
    n_chip = n_src // 2
    scale = LOG2E / (EPSILON * math.sqrt(depth))
    me = lax.axis_index("src")
    ml = lax.axis_index("loop")
    chip = me // 2
    core = me % 2
    sib = chip * 2 + (1 - core)

    def at_src(s):
        return (s, ml)

    def peer(k):
        return lax.rem(me + k, n_src)

    def loop_peer(k):
        return lax.rem(ml + k, n_loop)

    tile_copy = pltpu.make_async_copy(tgt_ref, tiles, loc_sem.at[0])
    own_copy = pltpu.make_async_copy(src_ref, gather.at[me], loc_sem.at[1])
    tile_copy.start()
    own_copy.start()

    spot = lax.broadcasted_iota(jnp.int32, (1, 128), 1)
    for s in range(n_src):
        row = jnp.where(spot == slots, live_ref[0, s], 0)
        for c in range(slots):
            row = jnp.where(spot == c, lax.rem(list_ref[0, c, s], tiles_own), row)
        idpack_ref[s] = row
    ids_v[me] = idpack_ref[me]

    barrier = pltpu.get_barrier_semaphore()
    for k in range(1, n_src):
        pl.semaphore_signal(barrier, inc=1, device_id=(peer(k), ml), device_id_type=MESH)
    for k in range(1, n_loop):
        pl.semaphore_signal(barrier, inc=1, device_id=(me, loop_peer(k)), device_id_type=MESH)
    pl.semaphore_wait(barrier, n_src - 1 + n_loop - 1)

    def id_copy(to, slot):
        return pltpu.make_async_remote_copy(
            src_ref=idpack_ref.at[to], dst_ref=ids_v.at[slot],
            send_sem=id_send.at[to], recv_sem=id_recv.at[slot],
            device_id=at_src(to), device_id_type=MESH,
        )

    for k in range(1, n_src):
        id_copy(peer(k), me).start()

    def own_send(ch, lane, to):
        part = pl.ds(ch * chunk, chunk)
        return pltpu.make_async_remote_copy(
            src_ref=src_ref.at[part], dst_ref=gather.at[me, part],
            send_sem=gs_send.at[me, ch, lane], recv_sem=gs_recv.at[me, ch],
            device_id=at_src(to), device_id_type=MESH,
        )

    def pass_on(block, ch, lane, to):
        part = pl.ds(ch * chunk, chunk)
        return pltpu.make_async_remote_copy(
            src_ref=gather.at[block, part], dst_ref=gather.at[block, part],
            send_sem=gs_send.at[block, ch, lane], recv_sem=gs_recv.at[block, ch],
            device_id=at_src(to), device_id_type=MESH,
        )

    up = lax.rem(me + 2, n_src)
    down = lax.rem(me + n_src - 2, n_src)
    has_up = chip < n_chip - 1
    has_down = chip > 0
    for ch in range(CHUNKS):
        @pl.when(has_up)
        def _():
            own_send(ch, 0, up).start()

        @pl.when(has_down)
        def _():
            own_send(ch, 1, down).start()

    for ch in range(CHUNKS):
        own_send(ch, 2, sib).start()

    g_old = g_old_ref[...].astype(jnp.float32)
    for t in range(tiles_own):
        row = g_old[t : t + 1] * (LOG2E / EPSILON)
        gcol[t] = jnp.broadcast_to(row, (128, width)).T

    for k in range(1, n_src):
        id_copy(peer(k), peer(k)).wait_recv()
    to_smem = pltpu.make_async_copy(ids_v, ids_s, loc_sem.at[3])
    to_smem.start()
    to_smem.wait()
    tile_copy.wait()
    own_copy.wait()

    def row_copy(to, slot):
        return pltpu.make_async_remote_copy(
            src_ref=row_out.at[to], dst_ref=row_in.at[slot],
            send_sem=row_send.at[to], recv_sem=row_recv.at[slot],
            device_id=at_src(to), device_id_type=MESH,
        )

    def row_part(block, ch):
        part = pl.ds(pl.multiple_of(ch * chunk, chunk), chunk)
        rows_bf = gather[block, part, :]
        live = ids_s[block, 0, slots]
        best = None
        for c in range(slots):
            tid = ids_s[block, 0, c]
            dots = lax.dot_general(
                tiles[tid], rows_bf, (((1,), (1,)), ((), ())),
                preferred_element_type=jnp.float32,
            )
            g_rows = gcol[tid]
            vals = dots * scale + jnp.concatenate([g_rows] * (chunk // 128), axis=1)
            logits[block * slots + c, :, part] = vals
            top = jnp.max(vals, axis=0, keepdims=True)
            total = jnp.sum(jnp.exp2(vals - top), axis=0, keepdims=True)
            if c == 0:
                best, tot = top, total
            else:
                top = jnp.where(c < live, top, VERY_LOW)
                total = jnp.where(c < live, total, 0.0)
                new = jnp.maximum(best, top)
                tot = tot * jnp.exp2(best - new) + total * jnp.exp2(top - new)
                best = new
        row_out[block, 0:1, part] = best
        row_out[block, 1:2, part] = tot

    def own_step(ch, carry):
        row_part(me, ch)
        return carry

    lax.fori_loop(0, CHUNKS, own_step, 0)
    row_in[me] = row_out[me]

    def sib_step(ch, carry):
        pass_on(sib, ch, 2, sib).wait_recv()
        row_part(sib, ch)
        return carry

    lax.fori_loop(0, CHUNKS, sib_step, 0)
    row_copy(sib, me).start()

    def chip_chunks(k, first, last):
        low = chip - k
        high = chip + k

        def chunk_step(ch, carry):
            @pl.when(low >= 0)
            def _():
                block = low * 2 + core
                pass_on(block, ch, 0, up).wait_recv()

                @pl.when(has_up)
                def _():
                    pass_on(block, ch, 0, up).start()

                pass_on(block, ch, 2, sib).start()

            @pl.when(high < n_chip)
            def _():
                block = high * 2 + core
                pass_on(block, ch, 1, down).wait_recv()

                @pl.when(has_down)
                def _():
                    pass_on(block, ch, 1, down).start()

                pass_on(block, ch, 2, sib).start()

            def part_step(j, carry):
                other = jnp.where(j % 2 == 0, low, high)
                own_core = j < 2

                @pl.when((other >= 0) & (other < n_chip))
                def _():
                    block = other * 2 + jnp.where(own_core, core, 1 - core)

                    @pl.when(jnp.logical_not(own_core))
                    def _():
                        pass_on(block, ch, 2, sib).wait_recv()

                    row_part(block, ch)

                    @pl.when(ch == CHUNKS - 1)
                    def _():
                        row_copy(block, me).start()

                return carry

            return lax.fori_loop(0, 4, part_step, carry)

        lax.fori_loop(first, last, chunk_step, 0)

    def chip_step(k, carry):
        chip_chunks(k, 0, CHUNKS)
        return carry

    lax.fori_loop(1, n_chip - 1, chip_step, 0)

    def f_copy(to, slot):
        return pltpu.make_async_remote_copy(
            src_ref=f_all.at[slot], dst_ref=f_all.at[slot],
            send_sem=f_send.at[to], recv_sem=f_recv.at[slot],
            device_id=at_src(to), device_id_type=MESH,
        )

    def potential():
        for k in range(1, n_src):
            row_copy(peer(k), peer(k)).wait_recv()
        tops = row_in[:, 0, :]
        best = jnp.max(tops, axis=0, keepdims=True)
        total = jnp.sum(row_in[:, 1, :] * jnp.exp2(tops - best), axis=0, keepdims=True)
        f_two = log_a_ref[...] * LOG2E - (best + jnp.log2(total))
        f_ref[...] = f_two * (EPSILON * LN2)
        f_all[me] = f_two
        for k in range(1, n_src):
            f_copy(peer(k), me).start()

    def wait_potential(blocks):
        for s in blocks:
            @pl.when(me != s)
            def _():
                f_copy(sib, s).wait_recv()

    n_pairs = n_src * slots
    band = 32
    lane = lax.broadcasted_iota(jnp.int32, (band, 128), 1)

    def columns(count, pair_of, fresh):
        def band_step(r, carry):
            at = pl.ds(pl.multiple_of(r * band, band), band)

            def pair_step(i, state):
                tops, sums = state
                p = pair_of(i)
                vals = logits[p, at, :] + f_all[p // slots]
                parts = [vals[:, i : i + 128] for i in range(0, rows, 128)]
                top = functools.reduce(jnp.maximum, parts)
                total = functools.reduce(jnp.add, [jnp.exp2(v - top) for v in parts])
                full = jnp.max(top, axis=1, keepdims=True)
                total = jnp.sum(total * jnp.exp2(top - full), axis=1, keepdims=True)
                return (jnp.where(lane == p, full, tops), jnp.where(lane == p, total, sums))

            if fresh:
                state = (jnp.zeros((band, 128), jnp.float32),) * 2
            else:
                state = (col_top[at, :], col_sum[at, :])
            tops, sums = lax.fori_loop(0, count, pair_step, state, unroll=4)
            col_top[at, :] = tops
            col_sum[at, :] = sums
            return carry

        lax.fori_loop(0, width // band, band_step, 0)

    inner = (chip > 0) & (chip < n_chip - 1)
    outer = jnp.logical_not(inner)
    edge = 2 * slots
    pl.when(inner)(potential)

    @pl.when(outer)
    def _():
        chip_chunks(n_chip - 1, 0, CHUNKS - 1)

    wait_potential(range(2, n_src - 2))
    columns(n_pairs - 2 * edge, lambda i: i + edge, True)

    @pl.when(outer)
    def _():
        chip_chunks(n_chip - 1, CHUNKS - 1, CHUNKS)
        potential()

    wait_potential([0, 1, n_src - 2, n_src - 1])
    columns(2 * edge, lambda i: i + (i // edge) * (n_pairs - 2 * edge), False)
    tops = col_top[...].T
    sums = col_sum[...].T
    index = lax.broadcasted_iota(jnp.int32, (tiles_own, width), 0)
    masks = []
    tile_top = jnp.full((tiles_own, width), VERY_LOW, jnp.float32)
    for p in range(n_pairs):
        block, c = p // slots, p % slots
        tid = jnp.where(c < ids_s[block, 0, slots], ids_s[block, 0, c], -1)
        mask = index == tid
        masks.append(mask)
        tile_top = jnp.maximum(tile_top, jnp.where(mask, tops[p : p + 1], VERY_LOW))
    tile_sum = jnp.zeros((tiles_own, width), jnp.float32)
    for p in range(n_pairs):
        term = sums[p : p + 1] * jnp.exp2(jnp.minimum(tops[p : p + 1] - tile_top, 0.0))
        tile_sum = tile_sum + jnp.where(masks[p], term, 0.0)

    loop_in[ml, 0] = tile_top
    loop_in[ml, 1] = tile_sum
    loop_out[0] = tile_top
    loop_out[1] = tile_sum

    def loop_copy(to, slot):
        return pltpu.make_async_remote_copy(
            src_ref=loop_out, dst_ref=loop_in.at[slot],
            send_sem=loop_send.at[to], recv_sem=loop_recv.at[slot],
            device_id=(me, to), device_id_type=MESH,
        )

    for k in range(1, n_loop):
        loop_copy(loop_peer(k), ml).start()
    for k in range(1, n_loop):
        loop_copy(loop_peer(k), loop_peer(k)).wait_recv()
    top = functools.reduce(jnp.maximum, [loop_in[i, 0] for i in range(n_loop)])
    total = functools.reduce(
        jnp.add, [loop_in[i, 1] * jnp.exp2(loop_in[i, 0] - top) for i in range(n_loop)]
    )
    g_ref[...] = (
        EPSILON * log_b_ref[...] - (EPSILON * LN2) * (top + jnp.log2(total)) + g_old
    )

    for k in range(1, n_loop):
        loop_copy(loop_peer(k), ml).wait_send()
    for k in range(1, n_src):
        f_copy(peer(k), me).wait_send()
        row_copy(peer(k), me).wait_send()
        id_copy(peer(k), me).wait_send()
    for ch in range(CHUNKS):
        @pl.when(has_up)
        def _():
            own_send(ch, 0, up).wait_send()

        @pl.when(has_down)
        def _():
            own_send(ch, 1, down).wait_send()

        own_send(ch, 2, sib).wait_send()

    def drain(k, carry):
        low = chip - k
        high = chip + k
        for ch in range(CHUNKS):
            @pl.when(low >= 0)
            def _():
                block = low * 2 + core

                @pl.when(has_up)
                def _():
                    pass_on(block, ch, 0, up).wait_send()

                pass_on(block, ch, 2, sib).wait_send()

            @pl.when(high < n_chip)
            def _():
                block = high * 2 + core

                @pl.when(has_down)
                def _():
                    pass_on(block, ch, 1, down).wait_send()

                pass_on(block, ch, 2, sib).wait_send()

        return carry

    lax.fori_loop(1, n_chip, drain, 0)


def local(sources, log_a, targets, g_old, log_b, tile_ids, live_count):
    n_src = lax.axis_size("src")
    n_loop = lax.axis_size("loop")
    rows, depth = sources.shape
    tiles_own, width = targets.shape[0], targets.shape[1]
    slots = tile_ids.shape[2]
    vmem = pl.BlockSpec(memory_space=pltpu.VMEM)
    hbm = pl.BlockSpec(memory_space=pl.ANY)
    smem = pl.BlockSpec(memory_space=pltpu.SMEM)
    dma = pltpu.SemaphoreType.DMA
    n_pairs = n_src * slots
    f_new, g_new = pl.pallas_call(
        functools.partial(fused, n_src, n_loop, slots),
        out_shape=(
            jax.ShapeDtypeStruct((1, rows), jnp.float32),
            jax.ShapeDtypeStruct((tiles_own, width), jnp.float32),
        ),
        in_specs=[hbm, hbm, vmem, vmem, vmem, smem, smem],
        out_specs=(vmem, vmem),
        scratch_shapes=[
            pltpu.VMEM((n_src, rows, depth), sources.dtype),
            pltpu.VMEM((tiles_own, width, depth), targets.dtype),
            pltpu.VMEM((n_pairs, width, rows), jnp.float32),
            pltpu.VMEM((tiles_own, width, 128), jnp.float32),
            pltpu.VMEM((n_src, 1, 128), jnp.int32),
            pltpu.VMEM((n_src, 1, 128), jnp.int32),
            pltpu.SMEM((n_src, 1, 128), jnp.int32),
            pltpu.VMEM((n_src, 2, rows), jnp.float32),
            pltpu.VMEM((n_src, 2, rows), jnp.float32),
            pltpu.VMEM((n_src, 1, rows), jnp.float32),
            pltpu.VMEM((width, 128), jnp.float32),
            pltpu.VMEM((width, 128), jnp.float32),
            pltpu.VMEM((2, tiles_own, width), jnp.float32),
            pltpu.VMEM((n_loop, 2, tiles_own, width), jnp.float32),
            dma((n_src, CHUNKS, 3)),
            dma((n_src, CHUNKS)),
            dma((n_src,)),
            dma((n_src,)),
            dma((n_src,)),
            dma((n_src,)),
            dma((n_src,)),
            dma((n_src,)),
            dma((n_loop,)),
            dma((n_loop,)),
            dma((4,)),
        ],
        compiler_params=pltpu.CompilerParams(
            collective_id=0, has_side_effects=True, vmem_limit_bytes=60 * 1024 * 1024
        ),
        cost_estimate=pl.CostEstimate(
            flops=2 * n_pairs * rows * width * depth,
            bytes_accessed=2 * (tiles_own * width + rows) * depth,
            transcendentals=2 * n_pairs * rows * width,
        ),
    )(
        sources,
        targets,
        log_a[None],
        g_old,
        log_b,
        jnp.swapaxes(tile_ids, 1, 2),
        live_count,
    )
    return (f_new[0], g_new)


def solution(mesh):
    return jax.shard_map(
        local,
        mesh=mesh,
        in_specs=(
            P(("src", "loop"), None),
            P(("src", "loop")),
            P("src", None, None),
            P("src", None),
            P("src", None),
            P(("src", "loop"), None, None),
            P(("src", "loop"), None),
        ),
        out_specs=(P(("src", "loop")), P("src", None)),
        check_vma=False,
    )
```

```python
import functools
import math

import jax
import jax.numpy as jnp
from jax import lax
from jax.experimental import pallas as pl
from jax.experimental.pallas import tpu as pltpu
from jax.sharding import PartitionSpec as P

EPSILON = 0.1
VERY_LOW = -1e30
LOG2E = math.log2(math.e)
LN2 = math.log(2.0)
CHUNKS = 4
MESH = pl.DeviceIdType.MESH


def fused(
    n_src, n_loop, slots,
    src_ref, tgt_ref, log_a_ref, g_old_ref, log_b_ref, list_ref, live_ref,
    f_ref, g_ref,
    gather, tiles, logits, gcol, idpack_ref, ids_v, ids_s, row_out, row_in, f_all,
    col_top, col_sum, loop_out, loop_in,
    gs_send, gs_recv, id_send, id_recv, row_send, row_recv, f_send, f_recv,
    loop_send, loop_recv, loc_sem,
):
    rows, depth = src_ref.shape
    tiles_own, width, _ = tgt_ref.shape
    chunk = rows // CHUNKS
    n_chip = n_src // 2
    scale = LOG2E / (EPSILON * math.sqrt(depth))
    me = lax.axis_index("src")
    ml = lax.axis_index("loop")
    chip = me // 2
    core = me % 2
    sib = chip * 2 + (1 - core)

    def at_src(s):
        return (s, ml)

    def peer(k):
        return lax.rem(me + k, n_src)

    def loop_peer(k):
        return lax.rem(ml + k, n_loop)

    tile_copy = pltpu.make_async_copy(tgt_ref, tiles, loc_sem.at[0])
    own_copy = pltpu.make_async_copy(src_ref, gather.at[me], loc_sem.at[1])
    tile_copy.start()
    own_copy.start()

    spot = lax.broadcasted_iota(jnp.int32, (1, 128), 1)
    for s in range(n_src):
        row = jnp.where(spot == slots, live_ref[0, s], 0)
        for c in range(slots):
            row = jnp.where(spot == c, lax.rem(list_ref[0, c, s], tiles_own), row)
        idpack_ref[s] = row
    ids_v[me] = idpack_ref[me]

    barrier = pltpu.get_barrier_semaphore()
    for k in range(1, n_src):
        pl.semaphore_signal(barrier, inc=1, device_id=(peer(k), ml), device_id_type=MESH)
    for k in range(1, n_loop):
        pl.semaphore_signal(barrier, inc=1, device_id=(me, loop_peer(k)), device_id_type=MESH)
    pl.semaphore_wait(barrier, n_src - 1 + n_loop - 1)

    def id_copy(to, slot):
        return pltpu.make_async_remote_copy(
            src_ref=idpack_ref.at[to], dst_ref=ids_v.at[slot],
            send_sem=id_send.at[to], recv_sem=id_recv.at[slot],
            device_id=at_src(to), device_id_type=MESH,
        )

    for k in range(1, n_src):
        id_copy(peer(k), me).start()

    def own_send(ch, lane, to):
        part = pl.ds(ch * chunk, chunk)
        return pltpu.make_async_remote_copy(
            src_ref=src_ref.at[part], dst_ref=gather.at[me, part],
            send_sem=gs_send.at[me, ch, lane], recv_sem=gs_recv.at[me, ch],
            device_id=at_src(to), device_id_type=MESH,
        )

    def pass_on(block, ch, lane, to):
        part = pl.ds(ch * chunk, chunk)
        return pltpu.make_async_remote_copy(
            src_ref=gather.at[block, part], dst_ref=gather.at[block, part],
            send_sem=gs_send.at[block, ch, lane], recv_sem=gs_recv.at[block, ch],
            device_id=at_src(to), device_id_type=MESH,
        )

    up = lax.rem(me + 2, n_src)
    down = lax.rem(me + n_src - 2, n_src)
    has_up = chip < n_chip - 1
    has_down = chip > 0
    for ch in range(CHUNKS):
        @pl.when(has_up)
        def _():
            own_send(ch, 0, up).start()

        @pl.when(has_down)
        def _():
            own_send(ch, 1, down).start()

    for ch in range(CHUNKS):
        own_send(ch, 2, sib).start()

    g_old = g_old_ref[...].astype(jnp.float32)
    for t in range(tiles_own):
        row = g_old[t : t + 1] * (LOG2E / EPSILON)
        gcol[t] = jnp.broadcast_to(row, (128, width)).T

    for k in range(1, n_src):
        id_copy(peer(k), peer(k)).wait_recv()
    to_smem = pltpu.make_async_copy(ids_v, ids_s, loc_sem.at[3])
    to_smem.start()
    to_smem.wait()
    tile_copy.wait()
    own_copy.wait()

    def row_copy(to, slot):
        return pltpu.make_async_remote_copy(
            src_ref=row_out.at[to], dst_ref=row_in.at[slot],
            send_sem=row_send.at[to], recv_sem=row_recv.at[slot],
            device_id=at_src(to), device_id_type=MESH,
        )

    def row_part(block, ch):
        part = pl.ds(pl.multiple_of(ch * chunk, chunk), chunk)
        rows_bf = gather[block, part, :]
        live = ids_s[block, 0, slots]
        best = None
        for c in range(slots):
            tid = ids_s[block, 0, c]
            dots = lax.dot_general(
                tiles[tid], rows_bf, (((1,), (1,)), ((), ())),
                preferred_element_type=jnp.float32,
            )
            g_rows = gcol[tid]
            vals = dots * scale + jnp.concatenate([g_rows] * (chunk // 128), axis=1)
            logits[block * slots + c, :, part] = vals
            top = jnp.max(vals, axis=0, keepdims=True)
            total = jnp.sum(jnp.exp2(vals - top), axis=0, keepdims=True)
            if c == 0:
                best, tot = top, total
            else:
                top = jnp.where(c < live, top, VERY_LOW)
                total = jnp.where(c < live, total, 0.0)
                new = jnp.maximum(best, top)
                tot = tot * jnp.exp2(best - new) + total * jnp.exp2(top - new)
                best = new
        row_out[block, 0:1, part] = best
        row_out[block, 1:2, part] = tot

    def own_step(ch, carry):
        row_part(me, ch)
        return carry

    lax.fori_loop(0, CHUNKS, own_step, 0)
    row_in[me] = row_out[me]

    def sib_step(ch, carry):
        pass_on(sib, ch, 2, sib).wait_recv()
        row_part(sib, ch)
        return carry

    lax.fori_loop(0, CHUNKS, sib_step, 0)
    row_copy(sib, me).start()

    def chip_chunks(k, first, last):
        low = chip - k
        high = chip + k

        def chunk_step(ch, carry):
            @pl.when(low >= 0)
            def _():
                block = low * 2 + core
                pass_on(block, ch, 0, up).wait_recv()

                @pl.when(has_up)
                def _():
                    pass_on(block, ch, 0, up).start()

                pass_on(block, ch, 2, sib).start()

            @pl.when(high < n_chip)
            def _():
                block = high * 2 + core
                pass_on(block, ch, 1, down).wait_recv()

                @pl.when(has_down)
                def _():
                    pass_on(block, ch, 1, down).start()

                pass_on(block, ch, 2, sib).start()

            def part_step(j, carry):
                other = jnp.where(j % 2 == 0, low, high)
                own_core = j < 2

                @pl.when((other >= 0) & (other < n_chip))
                def _():
                    block = other * 2 + jnp.where(own_core, core, 1 - core)

                    @pl.when(jnp.logical_not(own_core))
                    def _():
                        pass_on(block, ch, 2, sib).wait_recv()

                    row_part(block, ch)

                    @pl.when(ch == CHUNKS - 1)
                    def _():
                        row_copy(block, me).start()

                return carry

            return lax.fori_loop(0, 4, part_step, carry)

        lax.fori_loop(first, last, chunk_step, 0)

    def chip_step(k, carry):
        chip_chunks(k, 0, CHUNKS)
        return carry

    lax.fori_loop(1, n_chip - 1, chip_step, 0)

    def f_copy(to, slot):
        return pltpu.make_async_remote_copy(
            src_ref=f_all.at[slot], dst_ref=f_all.at[slot],
            send_sem=f_send.at[to], recv_sem=f_recv.at[slot],
            device_id=at_src(to), device_id_type=MESH,
        )

    def potential():
        for k in range(1, n_src):
            row_copy(peer(k), peer(k)).wait_recv()
        tops = row_in[:, 0, :]
        best = jnp.max(tops, axis=0, keepdims=True)
        total = jnp.sum(row_in[:, 1, :] * jnp.exp2(tops - best), axis=0, keepdims=True)
        f_two = log_a_ref[...] * LOG2E - (best + jnp.log2(total))
        f_ref[...] = f_two * (EPSILON * LN2)
        f_all[me] = f_two
        for k in range(1, n_src):
            f_copy(peer(k), me).start()

    def wait_potential(blocks):
        for s in blocks:
            @pl.when(me != s)
            def _():
                f_copy(sib, s).wait_recv()

    n_pairs = n_src * slots
    band = 32
    lane = lax.broadcasted_iota(jnp.int32, (band, 128), 1)

    def columns(count, pair_of, fresh):
        def band_step(r, carry):
            at = pl.ds(pl.multiple_of(r * band, band), band)

            def pair_step(i, state):
                tops, sums = state
                p = pair_of(i)
                vals = logits[p, at, :] + f_all[p // slots]
                parts = [vals[:, i : i + 128] for i in range(0, rows, 128)]
                top = functools.reduce(jnp.maximum, parts)
                total = functools.reduce(jnp.add, [jnp.exp2(v - top) for v in parts])
                full = jnp.max(top, axis=1, keepdims=True)
                total = jnp.sum(total * jnp.exp2(top - full), axis=1, keepdims=True)
                return (jnp.where(lane == p, full, tops), jnp.where(lane == p, total, sums))

            if fresh:
                state = (jnp.zeros((band, 128), jnp.float32),) * 2
            else:
                state = (col_top[at, :], col_sum[at, :])
            tops, sums = lax.fori_loop(0, count, pair_step, state, unroll=4)
            col_top[at, :] = tops
            col_sum[at, :] = sums
            return carry

        lax.fori_loop(0, width // band, band_step, 0)

    inner = (chip > 0) & (chip < n_chip - 1)
    outer = jnp.logical_not(inner)
    edge = 2 * slots
    pl.when(inner)(potential)

    @pl.when(outer)
    def _():
        chip_chunks(n_chip - 1, 0, CHUNKS - 1)

    wait_potential(range(2, n_src - 2))
    columns(n_pairs - 2 * edge, lambda i: i + edge, True)

    @pl.when(outer)
    def _():
        chip_chunks(n_chip - 1, CHUNKS - 1, CHUNKS)
        potential()

    wait_potential([0, 1, n_src - 2, n_src - 1])
    columns(2 * edge, lambda i: i + (i // edge) * (n_pairs - 2 * edge), False)
    tops = col_top[...].T
    sums = col_sum[...].T
    index = lax.broadcasted_iota(jnp.int32, (tiles_own, width), 0)
    masks = []
    tile_top = jnp.full((tiles_own, width), VERY_LOW, jnp.float32)
    for p in range(n_pairs):
        block, c = p // slots, p % slots
        tid = jnp.where(c < ids_s[block, 0, slots], ids_s[block, 0, c], -1)
        mask = index == tid
        masks.append(mask)
        tile_top = jnp.maximum(tile_top, jnp.where(mask, tops[p : p + 1], VERY_LOW))
    tile_sum = jnp.zeros((tiles_own, width), jnp.float32)
    for p in range(n_pairs):
        term = sums[p : p + 1] * jnp.exp2(jnp.minimum(tops[p : p + 1] - tile_top, 0.0))
        tile_sum = tile_sum + jnp.where(masks[p], term, 0.0)

    loop_in[ml, 0] = tile_top
    loop_in[ml, 1] = tile_sum
    loop_out[0] = tile_top
    loop_out[1] = tile_sum

    def loop_copy(to, slot):
        return pltpu.make_async_remote_copy(
            src_ref=loop_out, dst_ref=loop_in.at[slot],
            send_sem=loop_send.at[to], recv_sem=loop_recv.at[slot],
            device_id=(me, to), device_id_type=MESH,
        )

    for k in range(1, n_loop):
        loop_copy(loop_peer(k), ml).start()
    for k in range(1, n_loop):
        loop_copy(loop_peer(k), loop_peer(k)).wait_recv()
    top = functools.reduce(jnp.maximum, [loop_in[i, 0] for i in range(n_loop)])
    total = functools.reduce(
        jnp.add, [loop_in[i, 1] * jnp.exp2(loop_in[i, 0] - top) for i in range(n_loop)]
    )
    g_ref[...] = (
        EPSILON * log_b_ref[...] - (EPSILON * LN2) * (top + jnp.log2(total)) + g_old
    )

    for k in range(1, n_loop):
        loop_copy(loop_peer(k), ml).wait_send()
    for k in range(1, n_src):
        f_copy(peer(k), me).wait_send()
        row_copy(peer(k), me).wait_send()
        id_copy(peer(k), me).wait_send()
    for ch in range(CHUNKS):
        @pl.when(has_up)
        def _():
            own_send(ch, 0, up).wait_send()

        @pl.when(has_down)
        def _():
            own_send(ch, 1, down).wait_send()

        own_send(ch, 2, sib).wait_send()

    def drain(k, carry):
        low = chip - k
        high = chip + k
        for ch in range(CHUNKS):
            @pl.when(low >= 0)
            def _():
                block = low * 2 + core

                @pl.when(has_up)
                def _():
                    pass_on(block, ch, 0, up).wait_send()

                pass_on(block, ch, 2, sib).wait_send()

            @pl.when(high < n_chip)
            def _():
                block = high * 2 + core

                @pl.when(has_down)
                def _():
                    pass_on(block, ch, 1, down).wait_send()

                pass_on(block, ch, 2, sib).wait_send()

        return carry

    lax.fori_loop(1, n_chip, drain, 0)


def hand_on(f_in, g_in, f_ref, g_ref):
    f_ref[...] = f_in[...]
    g_ref[...] = g_in[...]


def local(sources, log_a, targets, g_old, log_b, tile_ids, live_count):
    n_src = lax.axis_size("src")
    n_loop = lax.axis_size("loop")
    rows, depth = sources.shape
    tiles_own, width = targets.shape[0], targets.shape[1]
    slots = tile_ids.shape[2]
    vmem = pl.BlockSpec(memory_space=pltpu.VMEM)
    hbm = pl.BlockSpec(memory_space=pl.ANY)
    smem = pl.BlockSpec(memory_space=pltpu.SMEM)
    dma = pltpu.SemaphoreType.DMA
    n_pairs = n_src * slots
    f_new, g_new = pl.pallas_call(
        functools.partial(fused, n_src, n_loop, slots),
        out_shape=(
            jax.ShapeDtypeStruct((1, rows), jnp.float32),
            jax.ShapeDtypeStruct((tiles_own, width), jnp.float32),
        ),
        in_specs=[hbm, hbm, vmem, vmem, vmem, smem, smem],
        out_specs=(vmem, vmem),
        scratch_shapes=[
            pltpu.VMEM((n_src, rows, depth), sources.dtype),
            pltpu.VMEM((tiles_own, width, depth), targets.dtype),
            pltpu.VMEM((n_pairs, width, rows), jnp.float32),
            pltpu.VMEM((tiles_own, width, 128), jnp.float32),
            pltpu.VMEM((n_src, 1, 128), jnp.int32),
            pltpu.VMEM((n_src, 1, 128), jnp.int32),
            pltpu.SMEM((n_src, 1, 128), jnp.int32),
            pltpu.VMEM((n_src, 2, rows), jnp.float32),
            pltpu.VMEM((n_src, 2, rows), jnp.float32),
            pltpu.VMEM((n_src, 1, rows), jnp.float32),
            pltpu.VMEM((width, 128), jnp.float32),
            pltpu.VMEM((width, 128), jnp.float32),
            pltpu.VMEM((2, tiles_own, width), jnp.float32),
            pltpu.VMEM((n_loop, 2, tiles_own, width), jnp.float32),
            dma((n_src, CHUNKS, 3)),
            dma((n_src, CHUNKS)),
            dma((n_src,)),
            dma((n_src,)),
            dma((n_src,)),
            dma((n_src,)),
            dma((n_src,)),
            dma((n_src,)),
            dma((n_loop,)),
            dma((n_loop,)),
            dma((4,)),
        ],
        compiler_params=pltpu.CompilerParams(
            collective_id=0, has_side_effects=True, vmem_limit_bytes=60 * 1024 * 1024
        ),
        cost_estimate=pl.CostEstimate(
            flops=2 * n_pairs * rows * width * depth,
            bytes_accessed=2 * (tiles_own * width + rows) * depth,
            transcendentals=2 * n_pairs * rows * width,
        ),
    )(
        sources,
        targets,
        log_a[None],
        g_old,
        log_b,
        jnp.swapaxes(tile_ids, 1, 2),
        live_count,
    )
    f_new, g_new = pl.pallas_call(
        hand_on,
        out_shape=(
            jax.ShapeDtypeStruct((1, rows), jnp.float32),
            jax.ShapeDtypeStruct((tiles_own, width), jnp.float32),
        ),
        in_specs=[vmem, vmem],
        out_specs=(vmem, vmem),
    )(f_new, g_new)
    return (f_new[0], g_new)


def solution(mesh):
    return jax.shard_map(
        local,
        mesh=mesh,
        in_specs=(
            P(("src", "loop"), None),
            P(("src", "loop")),
            P("src", None, None),
            P("src", None),
            P("src", None),
            P(("src", "loop"), None, None),
            P(("src", "loop"), None),
        ),
        out_specs=(P(("src", "loop")), P("src", None)),
        check_vma=False,
    )
```

```python
import functools
import math

import jax
import jax.numpy as jnp
from jax import lax
from jax.experimental import pallas as pl
from jax.experimental.pallas import tpu as pltpu
from jax.sharding import PartitionSpec as P

EPSILON = 0.1
VERY_LOW = -1e30
LOG2E = math.log2(math.e)
LN2 = math.log(2.0)
CHUNKS = 2
MESH = pl.DeviceIdType.MESH


def fused(
    n_src, n_loop, slots,
    src_ref, tgt_ref, log_a_ref, g_old_ref, log_b_ref, list_ref, live_ref,
    f_ref, g_ref,
    gather, tiles, logits, gcol, idpack_ref, ids_v, ids_s, row_out, row_in, f_all,
    col_top, col_sum, loop_out, loop_in,
    gs_send, gs_recv, id_send, id_recv, row_send, row_recv, f_send, f_recv,
    loop_send, loop_recv, loc_sem,
):
    rows, depth = src_ref.shape
    tiles_own, width, _ = tgt_ref.shape
    chunk = rows // CHUNKS
    n_chip = n_src // 2
    scale = LOG2E / (EPSILON * math.sqrt(depth))
    me = lax.axis_index("src")
    ml = lax.axis_index("loop")
    chip = me // 2
    core = me % 2
    sib = chip * 2 + (1 - core)

    def at_src(s):
        return (s, ml)

    def peer(k):
        return lax.rem(me + k, n_src)

    def loop_peer(k):
        return lax.rem(ml + k, n_loop)

    tile_copy = pltpu.make_async_copy(tgt_ref, tiles, loc_sem.at[0])
    own_copy = pltpu.make_async_copy(src_ref, gather.at[me], loc_sem.at[1])
    tile_copy.start()
    own_copy.start()

    spot = lax.broadcasted_iota(jnp.int32, (1, 128), 1)
    for s in range(n_src):
        row = jnp.where(spot == slots, live_ref[0, s], 0)
        for c in range(slots):
            row = jnp.where(spot == c, lax.rem(list_ref[0, c, s], tiles_own), row)
        idpack_ref[s] = row
    ids_v[me] = idpack_ref[me]

    barrier = pltpu.get_barrier_semaphore()
    for k in range(1, n_src):
        pl.semaphore_signal(barrier, inc=1, device_id=(peer(k), ml), device_id_type=MESH)
    for k in range(1, n_loop):
        pl.semaphore_signal(barrier, inc=1, device_id=(me, loop_peer(k)), device_id_type=MESH)
    pl.semaphore_wait(barrier, n_src - 1 + n_loop - 1)

    def id_copy(to, slot):
        return pltpu.make_async_remote_copy(
            src_ref=idpack_ref.at[to], dst_ref=ids_v.at[slot],
            send_sem=id_send.at[to], recv_sem=id_recv.at[slot],
            device_id=at_src(to), device_id_type=MESH,
        )

    for k in range(1, n_src):
        id_copy(peer(k), me).start()

    def own_send(ch, lane, to):
        part = pl.ds(ch * chunk, chunk)
        return pltpu.make_async_remote_copy(
            src_ref=src_ref.at[part], dst_ref=gather.at[me, part],
            send_sem=gs_send.at[me, ch, lane], recv_sem=gs_recv.at[me, ch],
            device_id=at_src(to), device_id_type=MESH,
        )

    def pass_on(block, ch, lane, to):
        part = pl.ds(ch * chunk, chunk)
        return pltpu.make_async_remote_copy(
            src_ref=gather.at[block, part], dst_ref=gather.at[block, part],
            send_sem=gs_send.at[block, ch, lane], recv_sem=gs_recv.at[block, ch],
            device_id=at_src(to), device_id_type=MESH,
        )

    up = lax.rem(me + 2, n_src)
    down = lax.rem(me + n_src - 2, n_src)
    has_up = chip < n_chip - 1
    has_down = chip > 0
    for ch in range(CHUNKS):
        @pl.when(has_up)
        def _():
            own_send(ch, 0, up).start()

        @pl.when(has_down)
        def _():
            own_send(ch, 1, down).start()

    for ch in range(CHUNKS):
        own_send(ch, 2, sib).start()

    g_old = g_old_ref[...].astype(jnp.float32)
    for t in range(tiles_own):
        row = g_old[t : t + 1] * (LOG2E / EPSILON)
        gcol[t] = jnp.broadcast_to(row, (128, width)).T

    for k in range(1, n_src):
        id_copy(peer(k), peer(k)).wait_recv()
    to_smem = pltpu.make_async_copy(ids_v, ids_s, loc_sem.at[3])
    to_smem.start()
    to_smem.wait()
    tile_copy.wait()
    own_copy.wait()

    def row_copy(to, slot):
        return pltpu.make_async_remote_copy(
            src_ref=row_out.at[to], dst_ref=row_in.at[slot],
            send_sem=row_send.at[to], recv_sem=row_recv.at[slot],
            device_id=at_src(to), device_id_type=MESH,
        )

    def row_part(block, ch):
        part = pl.ds(pl.multiple_of(ch * chunk, chunk), chunk)
        rows_bf = gather[block, part, :]
        live = ids_s[block, 0, slots]
        best = None
        for c in range(slots):
            tid = ids_s[block, 0, c]
            dots = lax.dot_general(
                tiles[tid], rows_bf, (((1,), (1,)), ((), ())),
                preferred_element_type=jnp.float32,
            )
            g_rows = gcol[tid]
            vals = dots * scale + jnp.concatenate([g_rows] * (chunk // 128), axis=1)
            logits[block * slots + c, :, part] = vals
            top = jnp.max(vals, axis=0, keepdims=True)
            total = jnp.sum(jnp.exp2(vals - top), axis=0, keepdims=True)
            if c == 0:
                best, tot = top, total
            else:
                top = jnp.where(c < live, top, VERY_LOW)
                total = jnp.where(c < live, total, 0.0)
                new = jnp.maximum(best, top)
                tot = tot * jnp.exp2(best - new) + total * jnp.exp2(top - new)
                best = new
        row_out[block, 0:1, part] = best
        row_out[block, 1:2, part] = tot

    def own_step(ch, carry):
        row_part(me, ch)
        return carry

    lax.fori_loop(0, CHUNKS, own_step, 0)
    row_in[me] = row_out[me]

    def sib_step(ch, carry):
        pass_on(sib, ch, 2, sib).wait_recv()
        row_part(sib, ch)
        return carry

    lax.fori_loop(0, CHUNKS, sib_step, 0)
    row_copy(sib, me).start()

    def chip_chunks(k, first, last):
        low = chip - k
        high = chip + k

        def chunk_step(ch, carry):
            @pl.when(low >= 0)
            def _():
                block = low * 2 + core
                pass_on(block, ch, 0, up).wait_recv()

                @pl.when(has_up)
                def _():
                    pass_on(block, ch, 0, up).start()

                pass_on(block, ch, 2, sib).start()

            @pl.when(high < n_chip)
            def _():
                block = high * 2 + core
                pass_on(block, ch, 1, down).wait_recv()

                @pl.when(has_down)
                def _():
                    pass_on(block, ch, 1, down).start()

                pass_on(block, ch, 2, sib).start()

            def part_step(j, carry):
                other = jnp.where(j % 2 == 0, low, high)
                own_core = j < 2

                @pl.when((other >= 0) & (other < n_chip))
                def _():
                    block = other * 2 + jnp.where(own_core, core, 1 - core)

                    @pl.when(jnp.logical_not(own_core))
                    def _():
                        pass_on(block, ch, 2, sib).wait_recv()

                    row_part(block, ch)

                    @pl.when(ch == CHUNKS - 1)
                    def _():
                        row_copy(block, me).start()

                return carry

            return lax.fori_loop(0, 4, part_step, carry)

        lax.fori_loop(first, last, chunk_step, 0)

    def chip_step(k, carry):
        chip_chunks(k, 0, CHUNKS)
        return carry

    lax.fori_loop(1, n_chip - 1, chip_step, 0)

    def f_copy(to, slot):
        return pltpu.make_async_remote_copy(
            src_ref=f_all.at[slot], dst_ref=f_all.at[slot],
            send_sem=f_send.at[to], recv_sem=f_recv.at[slot],
            device_id=at_src(to), device_id_type=MESH,
        )

    def potential():
        for k in range(1, n_src):
            row_copy(peer(k), peer(k)).wait_recv()
        tops = row_in[:, 0, :]
        best = jnp.max(tops, axis=0, keepdims=True)
        total = jnp.sum(row_in[:, 1, :] * jnp.exp2(tops - best), axis=0, keepdims=True)
        f_two = log_a_ref[...] * LOG2E - (best + jnp.log2(total))
        f_ref[...] = f_two * (EPSILON * LN2)
        f_all[me] = f_two
        for k in range(1, n_src):
            f_copy(peer(k), me).start()

    def wait_potential(blocks):
        for s in blocks:
            @pl.when(me != s)
            def _():
                f_copy(sib, s).wait_recv()

    n_pairs = n_src * slots
    band = 32
    lane = lax.broadcasted_iota(jnp.int32, (band, 128), 1)

    def columns(count, pair_of, fresh):
        def band_step(r, carry):
            at = pl.ds(pl.multiple_of(r * band, band), band)

            def pair_step(i, state):
                tops, sums = state
                p = pair_of(i)
                vals = logits[p, at, :] + f_all[p // slots]
                parts = [vals[:, i : i + 128] for i in range(0, rows, 128)]
                top = functools.reduce(jnp.maximum, parts)
                total = functools.reduce(jnp.add, [jnp.exp2(v - top) for v in parts])
                full = jnp.max(top, axis=1, keepdims=True)
                total = jnp.sum(total * jnp.exp2(top - full), axis=1, keepdims=True)
                return (jnp.where(lane == p, full, tops), jnp.where(lane == p, total, sums))

            if fresh:
                state = (jnp.zeros((band, 128), jnp.float32),) * 2
            else:
                state = (col_top[at, :], col_sum[at, :])
            tops, sums = lax.fori_loop(0, count, pair_step, state, unroll=8)
            col_top[at, :] = tops
            col_sum[at, :] = sums
            return carry

        lax.fori_loop(0, width // band, band_step, 0)

    inner = (chip > 0) & (chip < n_chip - 1)
    outer = jnp.logical_not(inner)
    edge = 2 * slots
    pl.when(inner)(potential)

    @pl.when(outer)
    def _():
        chip_chunks(n_chip - 1, 0, CHUNKS - 1)

    wait_potential(range(2, n_src - 2))
    columns(n_pairs - 2 * edge, lambda i: i + edge, True)

    @pl.when(outer)
    def _():
        chip_chunks(n_chip - 1, CHUNKS - 1, CHUNKS)
        potential()

    wait_potential([0, 1, n_src - 2, n_src - 1])
    columns(2 * edge, lambda i: i + (i // edge) * (n_pairs - 2 * edge), False)
    tops = col_top[...].T
    sums = col_sum[...].T
    index = lax.broadcasted_iota(jnp.int32, (tiles_own, width), 0)
    masks = []
    tile_top = jnp.full((tiles_own, width), VERY_LOW, jnp.float32)
    for p in range(n_pairs):
        block, c = p // slots, p % slots
        tid = jnp.where(c < ids_s[block, 0, slots], ids_s[block, 0, c], -1)
        mask = index == tid
        masks.append(mask)
        tile_top = jnp.maximum(tile_top, jnp.where(mask, tops[p : p + 1], VERY_LOW))
    tile_sum = jnp.zeros((tiles_own, width), jnp.float32)
    for p in range(n_pairs):
        term = sums[p : p + 1] * jnp.exp2(jnp.minimum(tops[p : p + 1] - tile_top, 0.0))
        tile_sum = tile_sum + jnp.where(masks[p], term, 0.0)

    loop_in[ml, 0] = tile_top
    loop_in[ml, 1] = tile_sum
    loop_out[0] = tile_top
    loop_out[1] = tile_sum

    def loop_copy(to, slot):
        return pltpu.make_async_remote_copy(
            src_ref=loop_out, dst_ref=loop_in.at[slot],
            send_sem=loop_send.at[to], recv_sem=loop_recv.at[slot],
            device_id=(me, to), device_id_type=MESH,
        )

    for k in range(1, n_loop):
        loop_copy(loop_peer(k), ml).start()
    for k in range(1, n_loop):
        loop_copy(loop_peer(k), loop_peer(k)).wait_recv()
    top = functools.reduce(jnp.maximum, [loop_in[i, 0] for i in range(n_loop)])
    total = functools.reduce(
        jnp.add, [loop_in[i, 1] * jnp.exp2(loop_in[i, 0] - top) for i in range(n_loop)]
    )
    g_ref[...] = (
        EPSILON * log_b_ref[...] - (EPSILON * LN2) * (top + jnp.log2(total)) + g_old
    )

    for k in range(1, n_loop):
        loop_copy(loop_peer(k), ml).wait_send()
    for k in range(1, n_src):
        f_copy(peer(k), me).wait_send()
        row_copy(peer(k), me).wait_send()
        id_copy(peer(k), me).wait_send()
    for ch in range(CHUNKS):
        @pl.when(has_up)
        def _():
            own_send(ch, 0, up).wait_send()

        @pl.when(has_down)
        def _():
            own_send(ch, 1, down).wait_send()

        own_send(ch, 2, sib).wait_send()

    def drain(k, carry):
        low = chip - k
        high = chip + k
        for ch in range(CHUNKS):
            @pl.when(low >= 0)
            def _():
                block = low * 2 + core

                @pl.when(has_up)
                def _():
                    pass_on(block, ch, 0, up).wait_send()

                pass_on(block, ch, 2, sib).wait_send()

            @pl.when(high < n_chip)
            def _():
                block = high * 2 + core

                @pl.when(has_down)
                def _():
                    pass_on(block, ch, 1, down).wait_send()

                pass_on(block, ch, 2, sib).wait_send()

        return carry

    lax.fori_loop(1, n_chip, drain, 0)


def hand_on(f_in, g_in, f_ref, g_ref):
    f_ref[...] = f_in[...]
    g_ref[...] = g_in[...]


def local(sources, log_a, targets, g_old, log_b, tile_ids, live_count):
    n_src = lax.axis_size("src")
    n_loop = lax.axis_size("loop")
    rows, depth = sources.shape
    tiles_own, width = targets.shape[0], targets.shape[1]
    slots = tile_ids.shape[2]
    vmem = pl.BlockSpec(memory_space=pltpu.VMEM)
    hbm = pl.BlockSpec(memory_space=pl.ANY)
    smem = pl.BlockSpec(memory_space=pltpu.SMEM)
    dma = pltpu.SemaphoreType.DMA
    n_pairs = n_src * slots
    f_new, g_new = pl.pallas_call(
        functools.partial(fused, n_src, n_loop, slots),
        out_shape=(
            jax.ShapeDtypeStruct((1, rows), jnp.float32),
            jax.ShapeDtypeStruct((tiles_own, width), jnp.float32),
        ),
        in_specs=[hbm, hbm, vmem, vmem, vmem, smem, smem],
        out_specs=(vmem, vmem),
        scratch_shapes=[
            pltpu.VMEM((n_src, rows, depth), sources.dtype),
            pltpu.VMEM((tiles_own, width, depth), targets.dtype),
            pltpu.VMEM((n_pairs, width, rows), jnp.float32),
            pltpu.VMEM((tiles_own, width, 128), jnp.float32),
            pltpu.VMEM((n_src, 1, 128), jnp.int32),
            pltpu.VMEM((n_src, 1, 128), jnp.int32),
            pltpu.SMEM((n_src, 1, 128), jnp.int32),
            pltpu.VMEM((n_src, 2, rows), jnp.float32),
            pltpu.VMEM((n_src, 2, rows), jnp.float32),
            pltpu.VMEM((n_src, 1, rows), jnp.float32),
            pltpu.VMEM((width, 128), jnp.float32),
            pltpu.VMEM((width, 128), jnp.float32),
            pltpu.VMEM((2, tiles_own, width), jnp.float32),
            pltpu.VMEM((n_loop, 2, tiles_own, width), jnp.float32),
            dma((n_src, CHUNKS, 3)),
            dma((n_src, CHUNKS)),
            dma((n_src,)),
            dma((n_src,)),
            dma((n_src,)),
            dma((n_src,)),
            dma((n_src,)),
            dma((n_src,)),
            dma((n_loop,)),
            dma((n_loop,)),
            dma((4,)),
        ],
        compiler_params=pltpu.CompilerParams(
            collective_id=0, has_side_effects=True, vmem_limit_bytes=60 * 1024 * 1024
        ),
        cost_estimate=pl.CostEstimate(
            flops=2 * n_pairs * rows * width * depth,
            bytes_accessed=2 * (tiles_own * width + rows) * depth,
            transcendentals=2 * n_pairs * rows * width,
        ),
    )(
        sources,
        targets,
        log_a[None],
        g_old,
        log_b,
        jnp.swapaxes(tile_ids, 1, 2),
        live_count,
    )
    f_new, g_new = pl.pallas_call(
        hand_on,
        out_shape=(
            jax.ShapeDtypeStruct((1, rows), jnp.float32),
            jax.ShapeDtypeStruct((tiles_own, width), jnp.float32),
        ),
        in_specs=[vmem, vmem],
        out_specs=(vmem, vmem),
    )(f_new, g_new)
    return (f_new[0], g_new)


def solution(mesh):
    return jax.shard_map(
        local,
        mesh=mesh,
        in_specs=(
            P(("src", "loop"), None),
            P(("src", "loop")),
            P("src", None, None),
            P("src", None),
            P("src", None),
            P(("src", "loop"), None, None),
            P(("src", "loop"), None),
        ),
        out_specs=(P(("src", "loop")), P("src", None)),
        check_vma=False,
    )
```
